512 devices in a mesh: row: 16 (over y, core), ma: 32 (over x, z).
Axes of the slice: x: 4, y: 8, z: 8, core: 2. Of those that a mesh axis runs over, the one named last changes fastest.
Arguments:
- field_a: float32 [256, 2, 128, 384], P('row', None, 'ma'), may hold values from -6 to 6
- field_b: float32 [256, 2, 128, 384], P('row', None, 'ma'), may hold values from -6 to 6
- mode_ids: int32 [128], replicated, may hold values from 0 to 383, as said below
- legendre: bfloat16 [128, 384, 384], P('ma'), may hold values from -0.3125 to 0.3125
- quad_weights: float32 [384], replicated, may hold values from 0.4 to 1.2
- colat_cos: float32 [384], replicated, may hold values from -1 to 1
- lorentz: float32 [256, 384], P('row'), may hold values from 0.2 to 2
- theta_order: int32 [384], replicated, may hold values from 0 to 383, each once
- inverse: bfloat16 [384, 256, 256], P('row'), may hold values from -1 to 1
Outputs:
- new_a: float32 [256, 2, 128, 384], P('row', None, 'ma')
- new_b: float32 [256, 2, 128, 384], P('row', None, 'ma')
- zonal_mean: float32 [256, 384], P('row', 'ma')
The draws below stay inside these ranges and needn't reach their ends.
Inputs may be any that keep to these rules, and one draw needn't show every extreme that they name: `mode_ids`: for each k, entries 2k and 2k+1 are a mode m below 192 and its partner 384 - 1 - m; all entries differ; some pair holds mode 0. `theta_order`: every row index appears once.
All inputs are finite; a program needn't handle non-finite values.
Results may differ from the reference program's by a relative error of at most 0.03.
Values may be sent and summed in bfloat16 or wider, within the bound.
A program may use at most 128 MiB of HBM per device.

```python
import math
import jax
import jax.numpy as jnp
from jax import lax

NR = 256
L = 384
NTH = 384
NPHI = 768
STEPS = 3
M = 128


def draw_mode_ids(key, part):
    key = jax.random.fold_in(key, 11)
    low_modes = jax.random.permutation(key, L // 2)[:M // 2].astype(jnp.int32)
    low_modes = low_modes - jnp.min(low_modes)
    high_modes = L - 1 - low_modes
    return jnp.stack([low_modes, high_modes], axis=1).reshape(M).astype(jnp.int32)


def draw_inverse(key, part):
    key = jax.random.fold_in(key, 7)
    spread = jnp.clip(jax.random.normal(key, (L, NR, NR), jnp.float32), -4.0, 4.0) * (0.35 / NR ** 0.5)
    places = jnp.arange(NR, dtype=jnp.int32)
    diagonal_part = (places[:, None] == places[None, :]).astype(jnp.float32) * 0.7
    return (diagonal_part[None] + spread).astype(jnp.bfloat16)


def block_scale(key, dims, shards, low, high):
    loudness = 1.0
    for dim, shards_of in shards:
        steps = jax.random.uniform(jax.random.fold_in(jax.random.fold_in(key, 6), dim), (shards_of,), jnp.float32, low / len(shards), high / len(shards))
        loudness = loudness * jnp.repeat(jnp.exp(steps), dims[dim] // shards_of).reshape((-1,) + (1,) * (len(dims) - 1 - dim))
    return loudness


def gaussian(rng, extent, deviation, limit, shards=(), kind=jnp.bfloat16):
    result = deviation * jax.random.normal(rng, extent, jnp.float32)
    if shards:
        result = result * block_scale(rng, extent, shards, -0.22, 0.18)
    return jnp.clip(result, -limit, limit).astype(kind)


def setup_inputs(seed: int = 0) -> dict:
    key_list = jax.random.split(jax.random.key(seed), 10)
    return {
        "field_a": gaussian(key_list[0], (NR, 2, M, L), 1.0, 6.0, ((0, 16), (2, 32)), jnp.float32),
        "field_b": gaussian(key_list[1], (NR, 2, M, L), 1.0, 6.0, ((0, 16), (2, 32)), jnp.float32),
        "mode_ids": draw_mode_ids(jax.random.fold_in(key_list[9], 71), 0),
        "legendre": gaussian(key_list[3], (M, NTH, L), L ** -0.5, 0.3125, ((0, 32),)),
        "quad_weights": jnp.clip(jax.random.uniform(key_list[4], (NTH,), jnp.float32, 0.4, 1.2), 0.4, 1.2),
        "colat_cos": jnp.clip(jax.random.uniform(key_list[5], (NTH,), jnp.float32, -1.0, 1.0), -1.0, 1.0),
        "lorentz": jnp.clip(jnp.exp(math.log(2.0) - 2.3025851 * jax.random.uniform(key_list[6], (NR, NTH), jnp.float32) ** block_scale(key_list[6], (NR, NTH), ((0, 16),), -0.2, 0.2)), 0.2, 2.0),
        "theta_order": jax.random.permutation(key_list[7], NTH).astype(jnp.int32),
        "inverse": draw_inverse(jax.random.fold_in(key_list[9], 71), 0),
    }


step_size = 0.25

def phase_tables(mode_ids):
    mode_count = mode_ids.shape[0]
    points = jnp.arange(NPHI, dtype=jnp.int32)
    phase_steps = mode_ids[:, None] * points[None, :] % NPHI
    angles = phase_steps.astype(jnp.float32) * (2.0 * math.pi / NPHI)
    wave_rows = jnp.stack([jnp.cos(angles), -jnp.sin(angles)])
    synth_table = (wave_rows * (1.0 / math.sqrt(mode_count))).astype(jnp.bfloat16)
    back_table = (wave_rows * math.sqrt(2.0 / NPHI)).astype(jnp.bfloat16)
    return (synth_table, back_table)

def rounded(values):
    return lax.optimization_barrier(values.astype(jnp.bfloat16)).astype(jnp.float32)

def reference(field_a, field_b, mode_ids, legendre, quad_weights, colat_cos, lorentz, theta_order, inverse):
    degrees = jnp.arange(L, dtype=jnp.int32)
    live_mask = (degrees[None, :] >= mode_ids[:, None]).astype(jnp.float32)
    synth_table, back_table = phase_tables(mode_ids)
    synth_wide = synth_table.astype(jnp.float32)
    back_wide = back_table.astype(jnp.float32)
    table_wide = legendre.astype(jnp.float32)
    weighted = rounded(quad_weights[None, :, None] * table_wide)
    inverse_wide = inverse.astype(jnp.float32)
    spec_a = field_a * live_mask[None, None]
    spec_b = field_b * live_mask[None, None]
    blocks = NR // 8
    lorentz_blocks = lorentz.reshape(blocks, 8, NTH)
    coslat = colat_cos[None, :, None]

    def physical(pieces):
        grid_a, grid_b, lor_block = pieces
        phys_a = jnp.einsum('rcmt,cmp->rtp', grid_a, synth_wide)
        phys_b = jnp.einsum('rcmt,cmp->rtp', grid_b, synth_wide)
        force_a = 2.0 * coslat * phys_b + lor_block[:, :, None] * phys_a * phys_b
        force_b = phys_a * phys_b - 2.0 * coslat * phys_a
        modes_a = rounded(jnp.einsum('rtp,cmp->rcmt', rounded(force_a), back_wide))
        modes_b = rounded(jnp.einsum('rtp,cmp->rcmt', rounded(force_b), back_wide))
        return (modes_a, modes_b, lax.optimization_barrier(jnp.mean(force_a, axis=2)))
    block_shape = (blocks, 8, 2, M, NTH)
    for repeat in range(STEPS):
        grid_a = rounded(jnp.einsum('rcml,mtl->rcmt', rounded(spec_a), table_wide))
        grid_b = rounded(jnp.einsum('rcml,mtl->rcmt', rounded(spec_b), table_wide))
        modes_a, modes_b, zonal_part = lax.map(physical, (grid_a.reshape(block_shape), grid_b.reshape(block_shape), lorentz_blocks))
        modes_a = modes_a.reshape(NR, 2, M, NTH)
        modes_b = modes_b.reshape(NR, 2, M, NTH)
        zonal_full = zonal_part.reshape(NR, NTH)
        term_a = rounded(step_size * jnp.einsum('rcmt,mtl->rcml', modes_a, weighted))
        term_b = rounded(step_size * jnp.einsum('rcmt,mtl->rcml', modes_b, weighted))
        rhs_a = rounded(live_mask[None, None] * (spec_a + term_a))
        rhs_b = rounded(live_mask[None, None] * (spec_b + term_b))
        spec_a = jnp.einsum('lrs,scml->rcml', inverse_wide, rhs_a)
        spec_b = jnp.einsum('lrs,scml->rcml', inverse_wide, rhs_b)
    zonal_mean = jnp.take(zonal_full, theta_order, axis=1)
    return (spec_a, spec_b, zonal_mean)
```

```python
import math

import jax
import jax.numpy as jnp
from jax import lax
from jax.experimental import pallas as pl
from jax.experimental.pallas import tpu as pltpu
from jax.sharding import PartitionSpec as P

STEPS = 3
NPHI = 768
N = 384
NMA = 32
NROW = 16
F32 = jnp.float32
BF16 = jnp.bfloat16
MESH = pl.DeviceIdType.MESH


def iota(shape, dim):
    return lax.broadcasted_iota(jnp.int32, shape, dim)


def dot(a, b):
    return jnp.dot(a, b, preferred_element_type=F32)


def onehot(test):
    return jnp.where(test, 1.0, 0.0).astype(BF16)


def exact_dot(a, hot):
    hi = a.astype(BF16)
    rest = a - hi.astype(F32)
    mid = rest.astype(BF16)
    low = (rest - mid.astype(F32)).astype(BF16)
    return dot(hi, hot) + dot(mid, hot) + dot(low, hot)


def kernel(
    fa, fb, ids_s, theta_s, ids_v, theta_v, leg, qw, colat, lor, inv_hbm,
    out_a, out_b, out_z,
    legp, wp, spec, xs, tt, bt, val, k1, k2, force, yf, gs, g, ms, h, rs, c, us, s, inv, bf,
    send_sem, recv_sem, inv_sem,
):
    row = lax.axis_index("row")
    ma = lax.axis_index("ma")

    barrier = pltpu.get_barrier_semaphore()

    def greet_ma(i, _):
        pl.semaphore_signal(barrier, inc=1, device_id={"ma": lax.rem(ma + i, NMA)}, device_id_type=MESH)
        return 0

    def greet_row(i, _):
        pl.semaphore_signal(barrier, inc=1, device_id={"row": lax.rem(row + i, NROW)}, device_id_type=MESH)
        return 0

    lax.fori_loop(1, NMA, greet_ma, 0)
    lax.fori_loop(1, NROW, greet_row, 0)
    inv_copy = pltpu.make_async_copy(inv_hbm, inv, inv_sem)
    inv_copy.start()

    lane = iota((1, N), 1)
    lane128 = iota((1, 128), 1)
    degree = (lane & 15) * 24 + (lane >> 4)

    def live(m):
        return degree >= ids_s[ma * 4 + m]

    to_degree = onehot(iota((N, N), 0) == degree)
    nat = onehot(iota((N, N), 0) == theta_v[...])
    shuffle = onehot(iota((N, N), 0) == (lane & 31) * 12 + (lane >> 5))
    pick = jnp.transpose(dot(nat, shuffle)).astype(BF16)
    for m in range(4):
        legp[m] = dot(pick, dot(leg[m], to_degree).astype(BF16)).astype(BF16)

    for m in range(4):
        for part in range(2):
            for f, field in ((0, fa), (1, fb)):
                piece = field[:, part, m, :]
                hi = piece.astype(BF16)
                lo = (piece - hi.astype(F32)).astype(BF16)
                moved = jnp.where(live(m), dot(hi, to_degree) + dot(lo, to_degree), 0.0)
                spec[m * 4 + part * 2 + f] = moved
                xs[m * 4 + part * 2 + f] = moved.astype(BF16)

    pl.semaphore_wait(barrier, NMA + NROW - 2)

    def send(src, dst, count, axis, me, k):
        def one(i, _):
            to = lax.rem(me + i, count)
            pltpu.make_async_remote_copy(
                src_ref=src.at[to],
                dst_ref=dst.at[me],
                send_sem=send_sem.at[k],
                recv_sem=recv_sem.at[k],
                device_id={axis: to},
                device_id_type=MESH,
            ).start()
            return 0

        lax.fori_loop(1, count, one, 0)
        dst[me] = src[me]

    def arrive(src, dst, count, k):
        pltpu.make_async_copy(dst.at[pl.ds(0, count - 1)], dst.at[pl.ds(0, count - 1)], recv_sem.at[k]).wait()
        pltpu.make_async_copy(src.at[pl.ds(0, count - 1)], src.at[pl.ds(0, count - 1)], send_sem.at[k]).wait()

    def swap16(load, store):
        for q in range(3):
            cols = slice(q * 128, q * 128 + 128)
            parts = [load(i, cols) for i in range(16)]
            for k in (1, 2, 4, 8):
                low = (lane128 & k) == 0
                for i in range(16):
                    if i & k == 0:
                        a, b = parts[i], parts[i + k]
                        parts[i] = jnp.where(low, a, pltpu.roll(b, k, 1))
                        parts[i + k] = jnp.where(low, pltpu.roll(a, 128 - k, 1), b)
            for i in range(16):
                store(i, cols, parts[i])

    def prepare_longitude():
        n = iota((1, 256), 1)
        expand = onehot(iota((128, 256), 0) == (n >> 3) * 4 + (n & 3))
        ids = jnp.broadcast_to(ids_v[...], (8, 128))
        top = ids >> 4
        mode = 16.0 * dot(top.astype(F32).astype(BF16), expand) + dot((ids & 15).astype(F32).astype(BF16), expand)
        mode = mode[0:1]

        def angles(count, period):
            k = mode * iota((count, 256), 0).astype(F32)
            k = k - period * jnp.floor((k + 0.5) * (1.0 / period))
            k = jnp.where(k > period / 2, k - period, k)
            return k * (2.0 * math.pi / period)

        coarse = angles(24, 24)
        fine = angles(32, NPHI)
        cos_c, sin_c = jnp.cos(coarse), jnp.sin(coarse)
        cos_f, sin_f = jnp.cos(fine), jnp.sin(fine)
        is_cos = (n & 4) == 0
        lead_c = jnp.where(is_cos, cos_c, -sin_c)
        lead_s = jnp.where(is_cos, sin_c, cos_c)
        for a in range(24):
            value = lead_c[a:a + 1] * cos_f - lead_s[a:a + 1] * sin_f
            val[a * 32:a * 32 + 32, :] = value
            tt[a * 32:a * 32 + 32, :] = (value * (1.0 / math.sqrt(128))).astype(BF16)
        for a in range(3):
            bt[:, a * 256:a * 256 + 256] = (
                jnp.transpose(val[a * 256:a * 256 + 256, :]) * math.sqrt(2.0 / NPHI)
            ).astype(BF16)

        own = jnp.zeros((1, N), jnp.int32)
        for t in range(12):
            own = jnp.where((lane >> 5) == t, theta_s[ma * 12 + t], own)
        hot = onehot(iota((N, N), 0) == own)
        is_a = (lane & 16) == 0
        cosines = exact_dot(jnp.broadcast_to(colat[...], (8, N)), hot)[0:1]
        k1[...] = jnp.where(is_a, 2.0 * cosines, -2.0 * cosines)
        energy = exact_dot(lor[...], hot)
        energy = jnp.sum(jnp.where(iota((16, N), 0) == (lane & 15), energy, 0.0), axis=0, keepdims=True)
        k2[...] = jnp.where(is_a, energy, 1.0)

    def prepare_weighted():
        column = jnp.transpose(jnp.broadcast_to(qw[...], (128, N)))[:, 0:1]
        for m in range(4):
            w = (column * leg[m].astype(F32)).astype(BF16)
            w = dot(pick_ref[...], dot(w, to_degree).astype(BF16))
            wp[m] = jnp.where(live(m), w, 0.0).astype(BF16)

    pick_ref = bf.at[0:N, :]
    pick_ref[...] = pick

    def step(n, _):
        for m in range(4):
            x0 = xs[m * 4:m * 4 + 2].reshape(32, N)
            x1 = xs[m * 4 + 2:m * 4 + 4].reshape(32, N)
            x = jnp.concatenate([x0] * 4 + [x1] * 4, axis=0)
            y = lax.dot_general(legp[m], x, (((1,), (1,)), ((), ())), preferred_element_type=F32)
            for part in range(2):
                for q in range(3):
                    pieces = [
                        y[(4 * q + j) * 32:(4 * q + j) * 32 + 32, part * 128:part * 128 + 128] for j in range(4)
                    ]
                    piece = pieces[0]
                    for j in range(1, 4):
                        piece = jnp.where((lane128 >> 5) == j, pieces[j], piece)
                    yf[q, pl.ds(part * 4 + m, 32, stride=8), :] = piece
        for q in range(3):
            gs[:, :, q * 128:q * 128 + 128] = yf[q].reshape(NMA, 8, 128).astype(BF16)
        send(gs, g, NMA, "ma", ma, 0)
        pl.when(n == 0)(prepare_longitude)
        arrive(gs, g, NMA, 0)

        grid = g[...].astype(F32).reshape(256, N)
        swapped = []
        for q in range(3):
            piece = grid[:, q * 128:q * 128 + 128]
            swapped.append(
                jnp.where((lane128 & 16) == 0, pltpu.roll(piece, 112, 1), pltpu.roll(piece, 16, 1))
            )
        both = jnp.concatenate([grid] + swapped, axis=1).astype(BF16)
        total = jnp.zeros((1, N), F32)
        for a in range(3):
            phys = dot(tt[a * 256:a * 256 + 256, :], both)
            value = phys[:, N:] * (k1[...] + k2[...] * phys[:, :N])
            force[a * 256:a * 256 + 256, :] = value.astype(BF16)
            total = total + jnp.sum(value, axis=0, keepdims=True)
        out_z[...] = jnp.broadcast_to(total * (1.0 / NPHI), (8, N))
        ms[...] = dot(bt[...], force[...]).reshape(NMA, 8, N).astype(BF16)
        send(ms, h, NMA, "ma", ma, 1)
        pl.when(n == 0)(prepare_weighted)
        arrive(ms, h, NMA, 1)

        for q in range(3):
            yf[q] = h[:, :, q * 128:q * 128 + 128].astype(F32).reshape(256, 128)
        for m in range(4):
            pieces = []
            for t in range(12):
                q, j = t // 4, t % 4
                p0 = yf[q, pl.ds(m, 32, stride=8), :]
                p1 = yf[q, pl.ds(4 + m, 32, stride=8), :]
                if j != 0:
                    p0 = pltpu.roll(p0, 128 - 32 * j, 1)
                if j != 1:
                    p1 = pltpu.roll(p1, (160 - 32 * j) % 128, 1)
                pieces.append(jnp.where(lane128 < 32, p0, p1))
            z = jnp.transpose(jnp.concatenate(pieces, axis=0))[0:64].astype(BF16)
            term = (0.25 * dot(z, wp[m])).astype(BF16).astype(F32)
            val_rows = spec[m * 4:m * 4 + 4].reshape(64, N) + term
            spec[m * 4:m * 4 + 4] = val_rows.astype(BF16).astype(F32).reshape(4, 16, N)

        def put_rs(i, cols, v):
            rs[i, :, cols] = v.astype(BF16)

        swap16(lambda i, cols: spec[i, :, cols], put_rs)
        send(rs, c, NROW, "row", row, 2)
        pl.when(n == 0)(inv_copy.wait)
        arrive(rs, c, NROW, 2)

        for q in range(3):
            right = c[:, :, q * 128:q * 128 + 128].reshape(256, 128)
            solved = dot(inv[q * 8], right)
            for i in range(1, 8):
                solved = jnp.where((lane128 >> 4) == i, dot(inv[q * 8 + i], right), solved)
            us[:, :, q * 128:q * 128 + 128] = solved.astype(BF16).reshape(NROW, 16, 128)
        send(us, s, NROW, "row", row, 3)
        arrive(us, s, NROW, 3)

        def put_spec(i, cols, v):
            spec[i, :, cols] = v
            xs[i, :, cols] = v.astype(BF16)

        swap16(lambda i, cols: s[i, :, cols].astype(F32), put_spec)
        return 0

    lax.fori_loop(0, STEPS, step, 0)

    from_degree = onehot((iota((N, N), 0) & 15) * 24 + (iota((N, N), 0) >> 4) == iota((N, N), 1))
    result = dot(xs[...].reshape(256, N), from_degree)
    for m in range(4):
        for part in range(2):
            for f, out in ((0, out_a), (1, out_b)):
                i = m * 4 + part * 2 + f
                for q in range(3):
                    out[q, pl.ds(part * 4 + m, 16, stride=8), :] = result[i * 16:i * 16 + 16, q * 128:q * 128 + 128]


def shards(
    field_a, field_b, mode_ids, legendre, quad_weights, colat_cos, lorentz, theta_order, inverse
):
    vmem = pl.BlockSpec(memory_space=pltpu.VMEM)
    smem = pl.BlockSpec(memory_space=pltpu.SMEM)
    out_a, out_b, out_z = pl.pallas_call(
        kernel,
        out_shape=(
            jax.ShapeDtypeStruct((3, 128, 128), F32),
            jax.ShapeDtypeStruct((3, 128, 128), F32),
            jax.ShapeDtypeStruct((8, N), F32),
        ),
        in_specs=[vmem, vmem, smem, smem, vmem, vmem, vmem, vmem, vmem, vmem, pl.BlockSpec(memory_space=pl.ANY)],
        out_specs=(vmem, vmem, vmem),
        scratch_shapes=[
            pltpu.VMEM((4, N, N), BF16),
            pltpu.VMEM((4, N, N), BF16),
            pltpu.VMEM((16, 16, N), F32),
            pltpu.VMEM((16, 16, N), BF16),
            pltpu.VMEM((NPHI, 256), BF16),
            pltpu.VMEM((256, NPHI), BF16),
            pltpu.VMEM((NPHI, 256), F32),
            pltpu.VMEM((1, N), F32),
            pltpu.VMEM((1, N), F32),
            pltpu.VMEM((NPHI, N), BF16),
            pltpu.VMEM((3, 256, 128), F32),
            pltpu.VMEM((NMA, 8, N), BF16),
            pltpu.VMEM((NMA, 8, N), BF16),
            pltpu.VMEM((NMA, 8, N), BF16),
            pltpu.VMEM((NMA, 8, N), BF16),
            pltpu.VMEM((NROW, 16, N), BF16),
            pltpu.VMEM((NROW, 16, N), BF16),
            pltpu.VMEM((NROW, 16, N), BF16),
            pltpu.VMEM((NROW, 16, N), BF16),
            pltpu.VMEM((24, 256, 256), BF16),
            pltpu.VMEM((N, N), BF16),
            pltpu.SemaphoreType.DMA((4,)),
            pltpu.SemaphoreType.DMA((4,)),
            pltpu.SemaphoreType.DMA,
        ],
        compiler_params=pltpu.CompilerParams(
            collective_id=0, has_side_effects=True, vmem_limit_bytes=48 * 1024 * 1024
        ),
        name="shell_steps",
    )(
        field_a, field_b, mode_ids, theta_order, mode_ids.reshape(1, 128), theta_order.reshape(1, N),
        legendre, quad_weights.reshape(1, N), colat_cos.reshape(1, N), lorentz, inverse,
    )
    new_a = out_a.transpose(1, 0, 2).reshape(16, 2, 4, N)
    new_b = out_b.transpose(1, 0, 2).reshape(16, 2, 4, N)
    zonal = out_z[0].reshape(12, 2, 16)[:, 0, :].T
    return (new_a, new_b, zonal)


def solution(mesh):
    return jax.shard_map(
        shards,
        mesh=mesh,
        in_specs=(
            P("row", None, "ma", None),
            P("row", None, "ma", None),
            P(),
            P("ma", None, None),
            P(),
            P(),
            P("row", None),
            P(),
            P("row", None, None),
        ),
        out_specs=(P("row", None, "ma", None), P("row", None, "ma", None), P("row", "ma")),
        check_vma=False,
    )
```

```python
import math

import jax
import jax.numpy as jnp
from jax import lax
from jax.experimental import pallas as pl
from jax.experimental.pallas import tpu as pltpu
from jax.sharding import PartitionSpec as P

STEPS = 3
NPHI = 768
N = 384
NMA = 32
NROW = 16
F32 = jnp.float32
BF16 = jnp.bfloat16
MESH = pl.DeviceIdType.MESH


def iota(shape, dim):
    return lax.broadcasted_iota(jnp.int32, shape, dim)


def dot(a, b):
    return jnp.dot(a, b, preferred_element_type=F32)


def onehot(test):
    return jnp.where(test, 1.0, 0.0).astype(BF16)


def exact_dot(a, hot):
    hi = a.astype(BF16)
    rest = a - hi.astype(F32)
    mid = rest.astype(BF16)
    low = (rest - mid.astype(F32)).astype(BF16)
    return dot(hi, hot) + dot(mid, hot) + dot(low, hot)


def far_first(count):
    return sorted(range(count), key=lambda d: -min(d, count - d))


def farthest(first, second):
    pairs = [(a, b) for a in far_first(first) for b in far_first(second)]
    pairs.sort(key=lambda p: -min(p[0], first - p[0]) - min(p[1], second - p[1]))
    return pairs[:-1]


def kernel(
    fa_hbm, fb_hbm, ids_hbm, theta_hbm, leg_hbm, qw_hbm, colat_hbm, lor_hbm, inv_hbm,
    out_a, out_b, out_z,
    fa, fb, leg, lor, ids_s, theta_s, ids_v, theta_v, qw, colat,
    legp, wp, spec, xs, tt, bt, val, k1, k2, force, yf, zt, gs, g, ms, h, rs, c, us, s, inv, pick,
    send_sem, recv_sem, load_sem,
):
    row = lax.axis_index("row")
    ma = lax.axis_index("ma")
    ma_x, ma_z = ma // 8, lax.rem(ma, 8)
    row_y, row_core = row // 2, lax.rem(row, 2)
    on_x = [lax.rem(ma_x + d, 4) * 8 for d in range(4)]
    on_z = [lax.rem(ma_z + d, 8) for d in range(8)]
    on_y = [lax.rem(row_y + d, 8) * 2 for d in range(8)]
    on_core = [row_core, 1 - row_core]
    ma_others = [on_x[a] + on_z[b] for a, b in farthest(4, 8)]
    row_others = [on_y[a] + on_core[b] for a in far_first(8) for b in (1, 0) if (a, b) != (0, 0)]

    loads = [
        pltpu.make_async_copy(src, dst, load_sem.at[i])
        for i, (src, dst) in enumerate((
            (theta_hbm, theta_v), (leg_hbm, leg), (ids_hbm, ids_s), (fa_hbm, fa), (fb_hbm, fb), (theta_hbm, theta_s),
            (ids_hbm, ids_v), (colat_hbm, colat), (lor_hbm, lor), (qw_hbm, qw), (inv_hbm, inv),
        ))
    ]
    for load in loads:
        load.start()

    barrier = pltpu.get_barrier_semaphore()

    def greet_ma(i, _):
        pl.semaphore_signal(barrier, inc=1, device_id={"ma": lax.rem(ma + i, NMA)}, device_id_type=MESH)
        return 0

    def greet_row(i, _):
        pl.semaphore_signal(barrier, inc=1, device_id={"row": lax.rem(row + i, NROW)}, device_id_type=MESH)
        return 0

    lax.fori_loop(1, NMA, greet_ma, 0)
    lax.fori_loop(1, NROW, greet_row, 0)

    lane = iota((1, N), 1)
    lane128 = iota((1, 128), 1)
    degree = (lane & 15) * 24 + (lane >> 4)

    def live(m):
        return degree >= ids_s[ma * 4 + m]

    to_degree = onehot(iota((N, N), 0) == degree)
    shuffle = onehot(iota((N, N), 0) == (lane & 31) * 12 + (lane >> 5))
    loads[0].wait()
    nat = onehot(iota((N, N), 0) == theta_v[...].reshape(1, N))
    pick[...] = jnp.transpose(dot(nat, shuffle)).astype(BF16)
    loads[1].wait()
    for m in range(4):
        legp[m] = dot(pick[...], dot(leg[m], to_degree).astype(BF16)).astype(BF16)

    for load in loads[2:5]:
        load.wait()
    for m in range(4):
        for part in range(2):
            for f, field in ((0, fa), (1, fb)):
                piece = field[:, part, m, :]
                hi = piece.astype(BF16)
                lo = (piece - hi.astype(F32)).astype(BF16)
                moved = jnp.where(live(m), dot(hi, to_degree) + dot(lo, to_degree), 0.0)
                spec[m * 4 + part * 2 + f] = moved
                xs[m * 4 + part * 2 + f] = moved.astype(BF16)

    pl.semaphore_wait(barrier, NMA + NROW - 2)

    def cols(q):
        return slice(q * 128, q * 128 + 128)

    def send(src, dst, k, q, axis, me, others):
        for to in others:
            pltpu.make_async_remote_copy(
                src_ref=src.at[to, :, cols(q)],
                dst_ref=dst.at[me, :, cols(q)],
                send_sem=send_sem.at[k, q],
                recv_sem=recv_sem.at[k, q],
                device_id={axis: to},
                device_id_type=MESH,
            ).start()
        dst[me, :, cols(q)] = src[me, :, cols(q)]

    def send_ma(src, dst, k, q):
        send(src, dst, k, q, "ma", ma, ma_others)

    def send_row(src, dst, k, q):
        send(src, dst, k, q, "row", row, row_others)

    def arrive(dst, count, k, q):
        rest = dst.at[pl.ds(0, count - 1), :, cols(q)]
        pltpu.make_async_copy(rest, rest, recv_sem.at[k, q]).wait()

    def sent(src, count, k):
        for q in range(3):
            rest = src.at[pl.ds(0, count - 1), :, cols(q)]
            pltpu.make_async_copy(rest, rest, send_sem.at[k, q]).wait()

    def swap16(parts):
        parts = list(parts)
        for k in (1, 2, 4, 8):
            low = (lane128 & k) == 0
            for i in range(16):
                if i & k == 0:
                    a, b = parts[i], parts[i + k]
                    parts[i] = jnp.where(low, a, pltpu.roll(b, k, 1))
                    parts[i + k] = jnp.where(low, pltpu.roll(a, 128 - k, 1), b)
        return parts

    def prepare_longitude():
        for load in loads[5:9]:
            load.wait()
        n = iota((1, 256), 1)
        expand = onehot(iota((128, 256), 0) == (n >> 3) * 4 + (n & 3))
        ids = jnp.broadcast_to(ids_v[...].reshape(1, 128), (8, 128))
        top = ids >> 4
        mode = 16.0 * dot(top.astype(F32).astype(BF16), expand) + dot((ids & 15).astype(F32).astype(BF16), expand)
        mode = mode[0:1]

        def angles(count, period):
            k = mode * iota((count, 256), 0).astype(F32)
            k = k - period * jnp.floor((k + 0.5) * (1.0 / period))
            k = jnp.where(k > period / 2, k - period, k)
            return k * (2.0 * math.pi / period)

        coarse = angles(24, 24)
        fine = angles(32, NPHI)
        cos_c, sin_c = jnp.cos(coarse), jnp.sin(coarse)
        cos_f, sin_f = jnp.cos(fine), jnp.sin(fine)
        is_cos = (n & 4) == 0
        lead_c = jnp.where(is_cos, cos_c, -sin_c)
        lead_s = jnp.where(is_cos, sin_c, cos_c)
        for a in range(24):
            value = lead_c[a:a + 1] * cos_f - lead_s[a:a + 1] * sin_f
            val[a * 32:a * 32 + 32, :] = value
            tt[a * 32:a * 32 + 32, :] = (value * (1.0 / math.sqrt(128))).astype(BF16)
        for a in range(3):
            bt[:, a * 256:a * 256 + 256] = (
                jnp.transpose(val[a * 256:a * 256 + 256, :]) * math.sqrt(2.0 / NPHI)
            ).astype(BF16)

        own = jnp.zeros((1, N), jnp.int32)
        for t in range(12):
            own = jnp.where((lane >> 5) == t, theta_s[ma * 12 + t], own)
        hot = onehot(iota((N, N), 0) == own)
        is_a = (lane & 16) == 0
        cosines = exact_dot(jnp.broadcast_to(colat[...].reshape(1, N), (8, N)), hot)[0:1]
        k1[...] = jnp.where(is_a, 2.0 * cosines, -2.0 * cosines)
        energy = exact_dot(lor[...], hot)
        energy = jnp.sum(jnp.where(iota((16, N), 0) == (lane & 15), energy, 0.0), axis=0, keepdims=True)
        k2[...] = jnp.where(is_a, energy, 1.0)

    def prepare_weighted():
        loads[9].wait()
        column = jnp.transpose(jnp.broadcast_to(qw[...].reshape(1, N), (128, N)))[:, 0:1]
        for m in range(4):
            w = (column * leg[m].astype(F32)).astype(BF16)
            w = dot(pick[...], dot(w, to_degree).astype(BF16))
            wp[m] = jnp.where(live(m), w, 0.0).astype(BF16)

    def step(n, _):
        for q in range(3):
            for m in range(4):
                x0 = xs[m * 4:m * 4 + 2].reshape(32, N)
                x1 = xs[m * 4 + 2:m * 4 + 4].reshape(32, N)
                x = jnp.concatenate([x0] * 4 + [x1] * 4, axis=0)
                y = lax.dot_general(
                    legp[m, cols(q), :], x, (((1,), (1,)), ((), ())), preferred_element_type=F32
                )
                for part in range(2):
                    piece = y[0:32, cols(part)]
                    for j in range(1, 4):
                        piece = jnp.where((lane128 >> 5) == j, y[j * 32:j * 32 + 32, cols(part)], piece)
                    yf[q, pl.ds(part * 4 + m, 32, stride=8), :] = piece
            gs[:, :, cols(q)] = yf[q].reshape(NMA, 8, 128).astype(BF16)
            send_ma(gs, g, 0, q)
        pl.when(n == 0)(prepare_longitude)

        for q in range(3):
            arrive(g, NMA, 0, q)
            grid = g[:, :, cols(q)].astype(F32).reshape(256, 128)
            other = jnp.where((lane128 & 16) == 0, pltpu.roll(grid, 112, 1), pltpu.roll(grid, 16, 1))
            both = jnp.concatenate([grid, other], axis=1).astype(BF16)
            total = jnp.zeros((1, 128), F32)
            for a in range(3):
                phys = dot(tt[a * 256:a * 256 + 256, :], both)
                value = phys[:, 128:] * (k1[:, cols(q)] + k2[:, cols(q)] * phys[:, :128])
                force[a * 256:a * 256 + 256, cols(q)] = value.astype(BF16)
                total = total + jnp.sum(value, axis=0, keepdims=True)
            out_z[:, cols(q)] = jnp.broadcast_to(total * (1.0 / NPHI), (8, 128))
            ms[:, :, cols(q)] = dot(bt[...], force[:, cols(q)]).reshape(NMA, 8, 128).astype(BF16)
            send_ma(ms, h, 1, q)
        pl.when(n == 0)(prepare_weighted)

        for q in range(3):
            arrive(h, NMA, 1, q)
            yf[q] = h[:, :, cols(q)].astype(F32).reshape(256, 128)
            for m in range(4):
                pieces = []
                for j in range(4):
                    p0 = yf[q, pl.ds(m, 32, stride=8), :]
                    p1 = yf[q, pl.ds(4 + m, 32, stride=8), :]
                    if j != 0:
                        p0 = pltpu.roll(p0, 128 - 32 * j, 1)
                    if j != 1:
                        p1 = pltpu.roll(p1, (160 - 32 * j) % 128, 1)
                    pieces.append(jnp.where(lane128 < 32, p0, p1))
                zt[m, :, cols(q)] = jnp.transpose(jnp.concatenate(pieces, axis=0))[0:64].astype(BF16)
        sent(gs, NMA, 0)
        for q in range(3):
            parts = []
            for m in range(4):
                term = (0.25 * dot(zt[m], wp[m, :, cols(q)])).astype(BF16).astype(F32)
                total = spec[m * 4:m * 4 + 4, :, cols(q)].reshape(64, 128) + term
                total = total.astype(BF16).astype(F32)
                parts += [total[i * 16:i * 16 + 16] for i in range(4)]
            for i, part in enumerate(swap16(parts)):
                rs[i, :, cols(q)] = part.astype(BF16)
            send_row(rs, c, 2, q)
        sent(ms, NMA, 1)
        pl.when(n == 0)(loads[10].wait)

        for q in range(3):
            arrive(c, NROW, 2, q)
            right = c[:, :, cols(q)].reshape(256, 128)
            solved = dot(inv[q * 8], right)
            for i in range(1, 8):
                solved = jnp.where((lane128 >> 4) == i, dot(inv[q * 8 + i], right), solved)
            us[:, :, cols(q)] = solved.astype(BF16).reshape(NROW, 16, 128)
            send_row(us, s, 3, q)
        sent(rs, NROW, 2)
        for q in range(3):
            arrive(s, NROW, 3, q)
            for i, part in enumerate(swap16([s[i, :, cols(q)].astype(F32) for i in range(16)])):
                spec[i, :, cols(q)] = part
                xs[i, :, cols(q)] = part.astype(BF16)
        sent(us, NROW, 3)
        return 0

    lax.fori_loop(0, STEPS, step, 0)

    from_degree = onehot((iota((N, N), 0) & 15) * 24 + (iota((N, N), 0) >> 4) == iota((N, N), 1))
    result = dot(xs[...].reshape(256, N), from_degree)
    for m in range(4):
        for part in range(2):
            for f, out in ((0, out_a), (1, out_b)):
                i = m * 4 + part * 2 + f
                for q in range(3):
                    out[q, pl.ds(part * 4 + m, 16, stride=8), :] = result[i * 16:i * 16 + 16, cols(q)]


def shards(
    field_a, field_b, mode_ids, legendre, quad_weights, colat_cos, lorentz, theta_order, inverse
):
    vmem = pl.BlockSpec(memory_space=pltpu.VMEM)
    hbm = pl.BlockSpec(memory_space=pltpu.HBM)
    out_a, out_b, out_z = pl.pallas_call(
        kernel,
        out_shape=(
            jax.ShapeDtypeStruct((3, 128, 128), F32),
            jax.ShapeDtypeStruct((3, 128, 128), F32),
            jax.ShapeDtypeStruct((8, N), F32),
        ),
        in_specs=[hbm] * 9,
        out_specs=(vmem, vmem, vmem),
        scratch_shapes=[
            pltpu.VMEM((16, 2, 4, N), F32),
            pltpu.VMEM((16, 2, 4, N), F32),
            pltpu.VMEM((4, N, N), BF16),
            pltpu.VMEM((16, N), F32),
            pltpu.SMEM((128,), jnp.int32),
            pltpu.SMEM((N,), jnp.int32),
            pltpu.VMEM((128,), jnp.int32),
            pltpu.VMEM((N,), jnp.int32),
            pltpu.VMEM((N,), F32),
            pltpu.VMEM((N,), F32),
            pltpu.VMEM((4, N, N), BF16),
            pltpu.VMEM((4, N, N), BF16),
            pltpu.VMEM((16, 16, N), F32),
            pltpu.VMEM((16, 16, N), BF16),
            pltpu.VMEM((NPHI, 256), BF16),
            pltpu.VMEM((256, NPHI), BF16),
            pltpu.VMEM((NPHI, 256), F32),
            pltpu.VMEM((1, N), F32),
            pltpu.VMEM((1, N), F32),
            pltpu.VMEM((NPHI, N), BF16),
            pltpu.VMEM((3, 256, 128), F32),
            pltpu.VMEM((4, 64, N), BF16),
            pltpu.VMEM((NMA, 8, N), BF16),
            pltpu.VMEM((NMA, 8, N), BF16),
            pltpu.VMEM((NMA, 8, N), BF16),
            pltpu.VMEM((NMA, 8, N), BF16),
            pltpu.VMEM((NROW, 16, N), BF16),
            pltpu.VMEM((NROW, 16, N), BF16),
            pltpu.VMEM((NROW, 16, N), BF16),
            pltpu.VMEM((NROW, 16, N), BF16),
            pltpu.VMEM((24, 256, 256), BF16),
            pltpu.VMEM((N, N), BF16),
            pltpu.SemaphoreType.DMA((4, 3)),
            pltpu.SemaphoreType.DMA((4, 3)),
            pltpu.SemaphoreType.DMA((11,)),
        ],
        compiler_params=pltpu.CompilerParams(
            collective_id=0, has_side_effects=True, vmem_limit_bytes=64 * 1024 * 1024
        ),
        name="shell_steps",
    )(
        field_a, field_b, mode_ids, theta_order, legendre, quad_weights, colat_cos, lorentz, inverse,
    )
    new_a = out_a.transpose(1, 0, 2).reshape(16, 2, 4, N)
    new_b = out_b.transpose(1, 0, 2).reshape(16, 2, 4, N)
    zonal = out_z[0].reshape(12, 2, 16)[:, 0, :].T
    return (new_a, new_b, zonal)


def solution(mesh):
    return jax.shard_map(
        shards,
        mesh=mesh,
        in_specs=(
            P("row", None, "ma", None),
            P("row", None, "ma", None),
            P(),
            P("ma", None, None),
            P(),
            P(),
            P("row", None),
            P(),
            P("row", None, None),
        ),
        out_specs=(P("row", None, "ma", None), P("row", None, "ma", None), P("row", "ma")),
        check_vma=False,
    )
```

```python
import math

import jax
import jax.numpy as jnp
from jax import lax
from jax.experimental import pallas as pl
from jax.experimental.pallas import tpu as pltpu
from jax.sharding import PartitionSpec as P

STEPS = 3
NPHI = 768
N = 384
NMA = 32
NROW = 16
MA_PIECES = ((0, 1), (1, 3))
ROW_PIECES = ((0, 1), (1, 3))
F32 = jnp.float32
BF16 = jnp.bfloat16
MESH = pl.DeviceIdType.MESH


def iota(shape, dim):
    return lax.broadcasted_iota(jnp.int32, shape, dim)


def dot(a, b):
    return jnp.dot(a, b, preferred_element_type=F32)


def onehot(test):
    return jnp.where(test, 1.0, 0.0).astype(BF16)


def exact_dot(a, hot):
    hi = a.astype(BF16)
    rest = a - hi.astype(F32)
    mid = rest.astype(BF16)
    low = (rest - mid.astype(F32)).astype(BF16)
    return dot(hi, hot) + dot(mid, hot) + dot(low, hot)


def far_first(count):
    return sorted(range(count), key=lambda d: -min(d, count - d))


def farthest(first, second):
    pairs = [(a, b) for a in far_first(first) for b in far_first(second)]
    pairs.sort(key=lambda p: -min(p[0], first - p[0]) - min(p[1], second - p[1]))
    return pairs[:-1]


def kernel(
    fa_hbm, fb_hbm, ids_hbm, theta_hbm, leg_hbm, qw_hbm, colat_hbm, lor_hbm, inv_hbm,
    xs, out_z,
    fa, fb, leg, lor, ids_s, theta_s, ids_v, theta_v, qw, colat,
    legp, wp, spec, tt, bt, val, k1, k2, force, yf, zt, back, gs, g, ms, h, rs, c, us, s, inv, pick,
    send_sem, recv_sem, load_sem,
):
    row = lax.axis_index("row")
    ma = lax.axis_index("ma")
    ma_x, ma_z = ma // 8, lax.rem(ma, 8)
    row_y, row_core = row // 2, lax.rem(row, 2)
    on_x = [lax.rem(ma_x + d, 4) * 8 for d in range(4)]
    on_z = [lax.rem(ma_z + d, 8) for d in range(8)]
    on_y = [lax.rem(row_y + d, 8) * 2 for d in range(8)]
    on_core = [row_core, 1 - row_core]
    ma_others = [on_x[a] + on_z[b] for a, b in farthest(4, 8)]
    row_others = [on_y[a] + on_core[b] for a in far_first(8) for b in (1, 0) if (a, b) != (0, 0)]

    barrier = pltpu.get_barrier_semaphore()
    for to in ma_others:
        pl.semaphore_signal(barrier, inc=1, device_id={"ma": to}, device_id_type=MESH)
    for to in row_others:
        pl.semaphore_signal(barrier, inc=1, device_id={"row": to}, device_id_type=MESH)

    loads = [
        pltpu.make_async_copy(src, dst, load_sem.at[i])
        for i, (src, dst) in enumerate((
            (theta_hbm, theta_v), (leg_hbm, leg), (ids_hbm, ids_s), (fa_hbm, fa), (fb_hbm, fb), (theta_hbm, theta_s),
            (ids_hbm, ids_v), (colat_hbm, colat), (lor_hbm, lor), (qw_hbm, qw), (inv_hbm, inv),
        ))
    ]
    for load in loads:
        load.start()

    lane = iota((1, N), 1)
    lane128 = iota((1, 128), 1)
    degree = (lane & 15) * 24 + (lane >> 4)

    shuffle = onehot(iota((N, N), 0) == (lane & 31) * 12 + (lane >> 5))
    loads[0].wait()
    nat = onehot(iota((N, N), 0) == theta_v[...].reshape(1, N))
    pick[...] = jnp.transpose(dot(nat, shuffle)).astype(BF16)
    for load in loads[1:5]:
        load.wait()
    for m in range(4):
        legp[m] = dot(pick[...], leg[m]).astype(BF16)
        alive = lane >= ids_s[ma * 4 + m]
        for part in range(2):
            for f, field in ((0, fa), (1, fb)):
                xs[m * 4 + part * 2 + f] = jnp.where(alive, field[:, part, m, :], 0.0).astype(BF16)

    pl.semaphore_wait(barrier, NMA + NROW - 2)

    def cols(q):
        return slice(q * 128, q * 128 + 128)

    def columns(piece):
        return slice(piece[0] * 128, piece[1] * 128)

    def send(src, dst, k, i, axis, me, others, pieces):
        block = columns(pieces[i])
        for to in others:
            pltpu.make_async_remote_copy(
                src_ref=src.at[to, :, block],
                dst_ref=dst.at[me, :, block],
                send_sem=send_sem.at[k, i],
                recv_sem=recv_sem.at[k, i],
                device_id={axis: to},
                device_id_type=MESH,
            ).start()
        dst[me, :, block] = src[me, :, block]

    def send_ma(src, dst, k, i):
        send(src, dst, k, i, "ma", ma, ma_others, MA_PIECES)

    def send_row(src, dst, k, i):
        send(src, dst, k, i, "row", row, row_others, ROW_PIECES)

    def finish(ref, sem, piece):
        rest = ref.at[pl.ds(0, ref.shape[0] - 1), :, columns(piece)]
        pltpu.make_async_copy(rest, rest, sem).wait()

    def arrive(dst, k, i):
        finish(dst, recv_sem.at[k, i], (MA_PIECES if k < 2 else ROW_PIECES)[i])

    def sent(src, k):
        for i, piece in enumerate(MA_PIECES if k < 2 else ROW_PIECES):
            finish(src, send_sem.at[k, i], piece)

    def swap16(parts):
        parts = list(parts)
        for k in (1, 2, 4, 8):
            low = (lane128 & k) == 0
            for i in range(16):
                if i & k == 0:
                    a, b = parts[i], parts[i + k]
                    parts[i] = jnp.where(low, a, pltpu.roll(b, k, 1))
                    parts[i + k] = jnp.where(low, pltpu.roll(a, 128 - k, 1), b)
        return parts

    def to_degree():
        return onehot(iota((N, N), 0) == degree)

    def prepare_spectral():
        hot = to_degree()
        for m in range(4):
            legp[m] = dot(legp[m], hot).astype(BF16)
            alive = lane >= ids_s[ma * 4 + m]
            for part in range(2):
                for f, field in ((0, fa), (1, fb)):
                    piece = jnp.where(alive, field[:, part, m, :], 0.0)
                    hi = piece.astype(BF16)
                    lo = (piece - hi.astype(F32)).astype(BF16)
                    spec[m * 4 + part * 2 + f] = dot(hi, hot) + dot(lo, hot)

    def prepare_longitude():
        for load in loads[5:9]:
            load.wait()
        n = iota((1, 256), 1)
        expand = onehot(iota((128, 256), 0) == (n >> 3) * 4 + (n & 3))
        ids = jnp.broadcast_to(ids_v[...].reshape(1, 128), (8, 128))
        top = ids >> 4
        mode = 16.0 * dot(top.astype(F32).astype(BF16), expand) + dot((ids & 15).astype(F32).astype(BF16), expand)
        mode = mode[0:1]

        def angles(count, period):
            k = mode * iota((count, 256), 0).astype(F32)
            k = k - period * jnp.floor((k + 0.5) * (1.0 / period))
            k = jnp.where(k > period / 2, k - period, k)
            return k * (2.0 * math.pi / period)

        coarse = angles(24, 24)
        fine = angles(32, NPHI)
        cos_c, sin_c = jnp.cos(coarse), jnp.sin(coarse)
        cos_f, sin_f = jnp.cos(fine), jnp.sin(fine)
        is_cos = (n & 4) == 0
        lead_c = jnp.where(is_cos, cos_c, -sin_c)
        lead_s = jnp.where(is_cos, sin_c, cos_c)
        for a in range(24):
            value = lead_c[a:a + 1] * cos_f - lead_s[a:a + 1] * sin_f
            val[a * 32:a * 32 + 32, :] = value
            tt[a * 32:a * 32 + 32, :] = (value * (1.0 / math.sqrt(128))).astype(BF16)
        for a in range(3):
            bt[:, a * 256:a * 256 + 256] = (
                jnp.transpose(val[a * 256:a * 256 + 256, :]) * math.sqrt(2.0 / NPHI)
            ).astype(BF16)

        own = jnp.zeros((1, N), jnp.int32)
        for t in range(12):
            own = jnp.where((lane >> 5) == t, theta_s[ma * 12 + t], own)
        hot = onehot(iota((N, N), 0) == own)
        is_a = (lane & 16) == 0
        cosines = exact_dot(jnp.broadcast_to(colat[...].reshape(1, N), (8, N)), hot)[0:1]
        k1[...] = jnp.where(is_a, 2.0 * cosines, -2.0 * cosines)
        energy = exact_dot(lor[...], hot)
        energy = jnp.sum(jnp.where(iota((16, N), 0) == (lane & 15), energy, 0.0), axis=0, keepdims=True)
        k2[...] = jnp.where(is_a, energy, 1.0)

    def prepare_weighted():
        loads[9].wait()
        hot = to_degree()
        column = jnp.transpose(jnp.broadcast_to(qw[...].reshape(1, N), (128, N)))[:, 0:1]
        for m in range(4):
            w = (column * leg[m].astype(F32)).astype(BF16)
            w = dot(pick[...], dot(w, hot).astype(BF16))
            w = jnp.where(degree >= ids_s[ma * 4 + m], w, 0.0).astype(BF16)
            for t in range(12):
                wp[t * 128 + m * 32:t * 128 + m * 32 + 32, :] = w[t * 32:t * 32 + 32]

    zt[...] = jnp.zeros_like(zt)

    def step(n, _):
        for i, piece in enumerate(MA_PIECES):
            low, high = piece
            for m in range(4):
                x0 = xs[m * 4:m * 4 + 2].reshape(32, N)
                x1 = xs[m * 4 + 2:m * 4 + 4].reshape(32, N)
                x = jnp.concatenate([x0] * 4 + [x1] * 4, axis=0)
                y = lax.dot_general(
                    legp[m, columns(piece), :], x, (((1,), (1,)), ((), ())), preferred_element_type=F32
                )
                for part in range(2):
                    for q in range(low, high):
                        first = (q - low) * 128
                        block = y[first:first + 32, cols(part)]
                        for j in range(1, 4):
                            other = y[first + j * 32:first + j * 32 + 32, cols(part)]
                            block = jnp.where((lane128 >> 5) == j, other, block)
                        yf[q, pl.ds(part * 4 + m, 32, stride=8), :] = block
            for q in range(low, high):
                gs[:, :, cols(q)] = yf[q].reshape(NMA, 8, 128).astype(BF16)
            send_ma(gs, g, 0, i)
        pl.when(n == 0)(prepare_longitude)
        pl.when(n == 0)(prepare_spectral)

        for i, piece in enumerate(MA_PIECES):
            arrive(g, 0, i)
            width = (piece[1] - piece[0]) * 128
            block = columns(piece)
            grids = [g[:, :, cols(q)].astype(F32).reshape(256, 128) for q in range(*piece)]
            others = [
                jnp.where((lane128 & 16) == 0, pltpu.roll(v, 112, 1), pltpu.roll(v, 16, 1)) for v in grids
            ]
            both = jnp.concatenate(grids + others, axis=1).astype(BF16)
            total = jnp.zeros((1, width), F32)
            for a in range(3):
                phys = dot(tt[a * 256:a * 256 + 256, :], both)
                value = phys[:, width:] * (k1[:, block] + k2[:, block] * phys[:, :width])
                force[a * 256:a * 256 + 256, block] = value.astype(BF16)
                total = total + jnp.sum(value, axis=0, keepdims=True)
            out_z[:, block] = jnp.broadcast_to(total * (1.0 / NPHI), (8, width))
            ms[:, :, block] = dot(bt[...], force[:, block]).reshape(NMA, 8, width).astype(BF16)
            send_ma(ms, h, 1, i)
        pl.when(n == 0)(prepare_weighted)

        for i, piece in enumerate(MA_PIECES):
            arrive(h, 1, i)
            for q in range(*piece):
                yf[q] = h[:, :, cols(q)].astype(F32).reshape(256, 128)
                for part in range(2):
                    stack = [yf[q, pl.ds(part * 4 + m, 32, stride=8), :] for m in range(4)]
                    turned = jnp.transpose(jnp.concatenate(stack, axis=0)).astype(BF16)
                    for m in range(4):
                        for j in range(4):
                            first = (q * 4 + j) * 128 + m * 32
                            zt[m * 64 + part * 32:m * 64 + part * 32 + 32, first:first + 32] = (
                                turned[j * 32:j * 32 + 32, m * 32:m * 32 + 32]
                            )
            if i == 0:
                early = slice(0, piece[1] * 512)
                late = slice(piece[1] * 512, 1536)
                back[...] = dot(zt[:, early], wp[early, :])
        sent(gs, 0)
        for i, piece in enumerate(ROW_PIECES):
            block = columns(piece)
            width = (piece[1] - piece[0]) * 128
            term = (0.25 * (back[:, block] + dot(zt[:, late], wp[late, block]))).astype(BF16).astype(F32)
            total = (spec[:, :, block].reshape(256, width) + term).astype(BF16).astype(F32)
            for q in range(*piece):
                parts = [total[j * 16:j * 16 + 16, cols(q - piece[0])] for j in range(16)]
                for j, part in enumerate(swap16(parts)):
                    rs[j, :, cols(q)] = part.astype(BF16)
            send_row(rs, c, 2, i)
        sent(ms, 1)
        pl.when(n == 0)(loads[10].wait)

        for i, piece in enumerate(ROW_PIECES):
            arrive(c, 2, i)
            for q in range(*piece):
                right = c[:, :, cols(q)].reshape(256, 128)
                solved = dot(inv[q * 8], right)
                for j in range(1, 8):
                    solved = jnp.where((lane128 >> 4) == j, dot(inv[q * 8 + j], right), solved)
                us[:, :, cols(q)] = solved.astype(BF16).reshape(NROW, 16, 128)
            send_row(us, s, 3, i)
        sent(rs, 2)
        for i, piece in enumerate(ROW_PIECES):
            arrive(s, 3, i)
            for q in range(*piece):
                for j, part in enumerate(swap16([s[j, :, cols(q)].astype(F32) for j in range(16)])):
                    spec[j, :, cols(q)] = part
                    xs[j, :, cols(q)] = part.astype(BF16)
        sent(us, 3)
        return 0

    lax.fori_loop(0, STEPS, step, 0)


def unload_kernel(xs, z, out_a, out_b, out_z):
    from_degree = onehot((iota((N, N), 0) & 15) * 24 + (iota((N, N), 0) >> 4) == iota((N, N), 1))
    result = dot(xs[...].reshape(256, N), from_degree)
    for m in range(4):
        for part in range(2):
            for f, out in ((0, out_a), (1, out_b)):
                i = m * 4 + part * 2 + f
                out[:, part, m, :] = result[i * 16:i * 16 + 16]
    lane = iota((16, N), 1)
    spread = jnp.where((lane & 31) == iota((16, N), 0), jnp.broadcast_to(z[0:1, :], (16, N)), 0.0)
    out_z[...] = exact_dot(spread, onehot((iota((N, 12), 0) >> 5) == iota((N, 12), 1)))


def shards(
    field_a, field_b, mode_ids, legendre, quad_weights, colat_cos, lorentz, theta_order, inverse
):
    vmem = pl.BlockSpec(memory_space=pltpu.VMEM)
    hbm = pl.BlockSpec(memory_space=pltpu.HBM)
    xs, z = pl.pallas_call(
        kernel,
        out_shape=(
            jax.ShapeDtypeStruct((16, 16, N), BF16),
            jax.ShapeDtypeStruct((8, N), F32),
        ),
        in_specs=[hbm] * 9,
        out_specs=(vmem, vmem),
        scratch_shapes=[
            pltpu.VMEM((16, 2, 4, N), F32),
            pltpu.VMEM((16, 2, 4, N), F32),
            pltpu.VMEM((4, N, N), BF16),
            pltpu.VMEM((16, N), F32),
            pltpu.SMEM((128,), jnp.int32),
            pltpu.SMEM((N,), jnp.int32),
            pltpu.VMEM((128,), jnp.int32),
            pltpu.VMEM((N,), jnp.int32),
            pltpu.VMEM((N,), F32),
            pltpu.VMEM((N,), F32),
            pltpu.VMEM((4, N, N), BF16),
            pltpu.VMEM((1536, N), BF16),
            pltpu.VMEM((16, 16, N), F32),
            pltpu.VMEM((NPHI, 256), BF16),
            pltpu.VMEM((256, NPHI), BF16),
            pltpu.VMEM((NPHI, 256), F32),
            pltpu.VMEM((1, N), F32),
            pltpu.VMEM((1, N), F32),
            pltpu.VMEM((NPHI, N), BF16),
            pltpu.VMEM((3, 256, 128), F32),
            pltpu.VMEM((256, 1536), BF16),
            pltpu.VMEM((256, N), F32),
            pltpu.VMEM((NMA, 8, N), BF16),
            pltpu.VMEM((NMA, 8, N), BF16),
            pltpu.VMEM((NMA, 8, N), BF16),
            pltpu.VMEM((NMA, 8, N), BF16),
            pltpu.VMEM((NROW, 16, N), BF16),
            pltpu.VMEM((NROW, 16, N), BF16),
            pltpu.VMEM((NROW, 16, N), BF16),
            pltpu.VMEM((NROW, 16, N), BF16),
            pltpu.VMEM((24, 256, 256), BF16),
            pltpu.VMEM((N, N), BF16),
            pltpu.SemaphoreType.DMA((4, 3)),
            pltpu.SemaphoreType.DMA((4, 3)),
            pltpu.SemaphoreType.DMA((11,)),
        ],
        compiler_params=pltpu.CompilerParams(
            collective_id=0, has_side_effects=True, vmem_limit_bytes=64 * 1024 * 1024
        ),
        name="shell_steps",
    )(
        field_a, field_b, mode_ids, theta_order, legendre, quad_weights, colat_cos, lorentz, inverse,
    )
    return pl.pallas_call(
        unload_kernel,
        out_shape=(
            jax.ShapeDtypeStruct((16, 2, 4, N), F32),
            jax.ShapeDtypeStruct((16, 2, 4, N), F32),
            jax.ShapeDtypeStruct((16, 12), F32),
        ),
        in_specs=[vmem, vmem],
        out_specs=(vmem, vmem, vmem),
        compiler_params=pltpu.CompilerParams(vmem_limit_bytes=64 * 1024 * 1024),
        name="unload",
    )(xs, z)


def solution(mesh):
    return jax.shard_map(
        shards,
        mesh=mesh,
        in_specs=(
            P("row", None, "ma", None),
            P("row", None, "ma", None),
            P(),
            P("ma", None, None),
            P(),
            P(),
            P("row", None),
            P(),
            P("row", None, None),
        ),
        out_specs=(P("row", None, "ma", None), P("row", None, "ma", None), P("row", "ma")),
        check_vma=False,
    )
```

```python
import math

import jax
import jax.numpy as jnp
from jax import lax
from jax.experimental import pallas as pl
from jax.experimental.pallas import tpu as pltpu
from jax.sharding import PartitionSpec as P

STEPS = 3
NPHI = 768
N = 384
NMA = 32
NROW = 16
PIECES = (((0, 1), (1, 3)), ((0, 1), (1, 3)), ((0, 1), (1, 3)), ((0, 1), (1, 3)))
F32 = jnp.float32
BF16 = jnp.bfloat16
MESH = pl.DeviceIdType.MESH


def iota(shape, dim):
    return lax.broadcasted_iota(jnp.int32, shape, dim)


def dot(a, b):
    return jnp.dot(a, b, preferred_element_type=F32)


def degree_of(column):
    holder = -column & 15
    return holder * 24 + (column >> 7) * 8 + ((((column & 127) + holder) >> 4) & 7)


def onehot(test):
    return jnp.where(test, 1.0, 0.0).astype(BF16)


def exact_dot(a, hot):
    hi = a.astype(BF16)
    rest = a - hi.astype(F32)
    mid = rest.astype(BF16)
    low = (rest - mid.astype(F32)).astype(BF16)
    return dot(hi, hot) + dot(mid, hot) + dot(low, hot)


def far_first(count):
    return sorted(range(count), key=lambda d: -min(d, count - d))


def farthest(first, second):
    pairs = [(a, b) for a in far_first(first) for b in far_first(second)]
    pairs.sort(key=lambda p: -min(p[0], first - p[0]) - min(p[1], second - p[1]))
    return pairs[:-1]


def units(arriving, leaving):
    cuts = sorted({low for low, _ in arriving + leaving}) + [3]
    return list(zip(cuts, cuts[1:]))


def kernel(
    fa_hbm, fb_hbm, ids_hbm, theta_hbm, leg_hbm, qw_hbm, colat_hbm, lor_hbm, inv_hbm,
    xs, out_z,
    fa, fb, leg, lor, ids_s, theta_s, ids_v, theta_v, qw, colat,
    legp, wp, spec, tt, bt, val, k1, k2, force, yf, zt, back, gs, g, ms, h, rs, c, us, s, inv, pick,
    send_sem, recv_sem, load_sem,
):
    row = lax.axis_index("row")
    ma = lax.axis_index("ma")
    ma_x, ma_z = ma // 8, lax.rem(ma, 8)
    row_y, row_core = row // 2, lax.rem(row, 2)
    on_x = [lax.rem(ma_x + d, 4) * 8 for d in range(4)]
    on_z = [lax.rem(ma_z + d, 8) for d in range(8)]
    on_y = [lax.rem(row_y + d, 8) * 2 for d in range(8)]
    on_core = [row_core, 1 - row_core]
    ma_others = [on_x[a] + on_z[b] for a, b in farthest(4, 8)]
    row_others = [on_y[a] + on_core[b] for a in far_first(8) for b in (1, 0) if (a, b) != (0, 0)]

    barrier = pltpu.get_barrier_semaphore()
    for to in ma_others:
        pl.semaphore_signal(barrier, inc=1, device_id={"ma": to}, device_id_type=MESH)
    for to in row_others:
        pl.semaphore_signal(barrier, inc=1, device_id={"row": to}, device_id_type=MESH)

    loads = [
        pltpu.make_async_copy(src, dst, load_sem.at[i])
        for i, (src, dst) in enumerate((
            (theta_hbm, theta_v), (leg_hbm, leg), (ids_hbm, ids_s), (fa_hbm, fa), (fb_hbm, fb), (theta_hbm, theta_s),
            (ids_hbm, ids_v), (colat_hbm, colat), (lor_hbm, lor), (qw_hbm, qw), (inv_hbm, inv),
        ))
    ]
    for load in loads:
        load.start()

    lane = iota((1, N), 1)
    lane128 = iota((1, 128), 1)
    degree = degree_of(lane)

    shuffle = onehot(iota((N, N), 0) == (lane & 31) * 12 + (lane >> 5))
    loads[0].wait()
    nat = onehot(iota((N, N), 0) == theta_v[...].reshape(1, N))
    pick[...] = jnp.transpose(dot(nat, shuffle)).astype(BF16)
    for load in loads[1:5]:
        load.wait()
    for m in range(4):
        legp[m] = dot(pick[...], leg[m]).astype(BF16)
        alive = lane >= ids_s[ma * 4 + m]
        for part in range(2):
            for f, field in ((0, fa), (1, fb)):
                xs[m * 4 + part * 2 + f] = jnp.where(alive, field[:, part, m, :], 0.0).astype(BF16)

    pl.semaphore_wait(barrier, NMA + NROW - 2)

    def cols(q):
        return slice(q * 128, q * 128 + 128)

    def columns(piece):
        return slice(piece[0] * 128, piece[1] * 128)

    def send(src, dst, k, done):
        axis, me, others = ("ma", ma, ma_others) if k < 2 else ("row", row, row_others)
        for i, piece in enumerate(PIECES[k]):
            if piece[1] == done:
                block = columns(piece)
                for to in others:
                    pltpu.make_async_remote_copy(
                        src_ref=src.at[to, :, block],
                        dst_ref=dst.at[me, :, block],
                        send_sem=send_sem.at[k, i],
                        recv_sem=recv_sem.at[k, i],
                        device_id={axis: to},
                        device_id_type=MESH,
                    ).start()
                dst[me, :, block] = src[me, :, block]

    def finish(ref, sem, piece):
        rest = ref.at[pl.ds(0, ref.shape[0] - 1), :, columns(piece)]
        pltpu.make_async_copy(rest, rest, sem).wait()

    def arrive(dst, k, first):
        for i, piece in enumerate(PIECES[k]):
            if piece[0] == first:
                finish(dst, recv_sem.at[k, i], piece)

    def sent(src, k):
        for i, piece in enumerate(PIECES[k]):
            finish(src, send_sem.at[k, i], piece)

    def by_holder(parts):
        parts = [pltpu.roll(v, i, 1) if i else v for i, v in enumerate(parts)]
        for k in (1, 2, 4, 8):
            parts = [jnp.where((lane128 & k) == 0, parts[j], parts[(j + k) % 16]) for j in range(16)]
        return parts

    def by_component(parts):
        for k in (1, 2, 4, 8):
            parts = [jnp.where((lane128 & k) == 0, parts[i], parts[(i - k) % 16]) for i in range(16)]
        return [pltpu.roll(v, 128 - i, 1) if i else v for i, v in enumerate(parts)]

    def to_degree():
        return onehot(iota((N, N), 0) == degree)

    def prepare_spectral():
        hot = to_degree()
        for m in range(4):
            legp[m] = dot(legp[m], hot).astype(BF16)
            alive = lane >= ids_s[ma * 4 + m]
            for part in range(2):
                for f, field in ((0, fa), (1, fb)):
                    piece = jnp.where(alive, field[:, part, m, :], 0.0)
                    hi = piece.astype(BF16)
                    lo = (piece - hi.astype(F32)).astype(BF16)
                    spec[m * 4 + part * 2 + f] = dot(hi, hot) + dot(lo, hot)

    def prepare_longitude():
        for load in loads[5:9]:
            load.wait()
        n = iota((1, 256), 1)
        expand = onehot(iota((128, 256), 0) == (n >> 3) * 4 + (n & 3))
        ids = jnp.broadcast_to(ids_v[...].reshape(1, 128), (8, 128))
        top = ids >> 4
        mode = 16.0 * dot(top.astype(F32).astype(BF16), expand) + dot((ids & 15).astype(F32).astype(BF16), expand)
        mode = mode[0:1]

        def angles(count, period):
            k = mode * iota((count, 256), 0).astype(F32)
            k = k - period * jnp.floor((k + 0.5) * (1.0 / period))
            k = jnp.where(k > period / 2, k - period, k)
            return k * (2.0 * math.pi / period)

        coarse = angles(24, 24)
        fine = angles(32, NPHI)
        cos_c, sin_c = jnp.cos(coarse), jnp.sin(coarse)
        cos_f, sin_f = jnp.cos(fine), jnp.sin(fine)
        is_cos = (n & 4) == 0
        lead_c = jnp.where(is_cos, cos_c, -sin_c)
        lead_s = jnp.where(is_cos, sin_c, cos_c)
        for a in range(24):
            value = lead_c[a:a + 1] * cos_f - lead_s[a:a + 1] * sin_f
            val[a * 32:a * 32 + 32, :] = value
            tt[a * 32:a * 32 + 32, :] = (value * (1.0 / math.sqrt(128))).astype(BF16)
        for a in range(3):
            bt[:, a * 256:a * 256 + 256] = (
                jnp.transpose(val[a * 256:a * 256 + 256, :]) * math.sqrt(2.0 / NPHI)
            ).astype(BF16)

        own = jnp.zeros((1, N), jnp.int32)
        for t in range(12):
            own = jnp.where((lane >> 5) == t, theta_s[ma * 12 + t], own)
        hot = onehot(iota((N, N), 0) == own)
        is_a = (lane & 16) == 0
        cosines = exact_dot(jnp.broadcast_to(colat[...].reshape(1, N), (8, N)), hot)[0:1]
        k1[...] = jnp.where(is_a, 2.0 * cosines, -2.0 * cosines)
        energy = exact_dot(lor[...], hot)
        energy = jnp.sum(jnp.where(iota((16, N), 0) == (lane & 15), energy, 0.0), axis=0, keepdims=True)
        k2[...] = jnp.where(is_a, energy, 1.0)

    def prepare_weighted():
        loads[9].wait()
        hot = to_degree()
        column = jnp.transpose(jnp.broadcast_to(qw[...].reshape(1, N), (128, N)))[:, 0:1]
        for m in range(4):
            w = (column * leg[m].astype(F32)).astype(BF16)
            w = dot(pick[...], dot(w, hot).astype(BF16))
            w = jnp.where(degree >= ids_s[ma * 4 + m], w, 0.0).astype(BF16)
            for t in range(12):
                wp[t * 128 + m * 32:t * 128 + m * 32 + 32, :] = w[t * 32:t * 32 + 32]

    zt[...] = jnp.zeros_like(zt)

    def step(n, _):
        for piece in PIECES[0]:
            low, high = piece
            for m in range(4):
                x0 = xs[m * 4:m * 4 + 2].reshape(32, N)
                x1 = xs[m * 4 + 2:m * 4 + 4].reshape(32, N)
                x = jnp.concatenate([x0] * 4 + [x1] * 4, axis=0)
                y = lax.dot_general(
                    legp[m, columns(piece), :], x, (((1,), (1,)), ((), ())), preferred_element_type=F32
                )
                for part in range(2):
                    for q in range(low, high):
                        first = (q - low) * 128
                        block = y[first:first + 32, cols(part)]
                        for j in range(1, 4):
                            other = y[first + j * 32:first + j * 32 + 32, cols(part)]
                            block = jnp.where((lane128 >> 5) == j, other, block)
                        yf[q, pl.ds(part * 4 + m, 32, stride=8), :] = block
            for q in range(low, high):
                gs[:, :, cols(q)] = yf[q].reshape(NMA, 8, 128).astype(BF16)
            send(gs, g, 0, high)
        pl.when(n == 0)(prepare_longitude)
        pl.when(n == 0)(prepare_spectral)

        for piece in units(PIECES[0], PIECES[1]):
            arrive(g, 0, piece[0])
            width = (piece[1] - piece[0]) * 128
            block = columns(piece)
            grids = [g[:, :, cols(q)].astype(F32).reshape(256, 128) for q in range(*piece)]
            others = [
                jnp.where((lane128 & 16) == 0, pltpu.roll(v, 112, 1), pltpu.roll(v, 16, 1)) for v in grids
            ]
            both = jnp.concatenate(grids + others, axis=1).astype(BF16)
            total = jnp.zeros((1, width), F32)
            for a in range(3):
                phys = dot(tt[a * 256:a * 256 + 256, :], both)
                value = phys[:, width:] * (k1[:, block] + k2[:, block] * phys[:, :width])
                force[a * 256:a * 256 + 256, block] = value.astype(BF16)
                total = total + jnp.sum(value, axis=0, keepdims=True)
            out_z[:, block] = jnp.broadcast_to(total * (1.0 / NPHI), (8, width))
            ms[:, :, block] = dot(bt[...], force[:, block]).reshape(NMA, 8, width).astype(BF16)
            send(ms, h, 1, piece[1])
        pl.when(n == 0)(prepare_weighted)

        for i, piece in enumerate(PIECES[1]):
            arrive(h, 1, piece[0])
            for q in range(*piece):
                yf[q] = h[:, :, cols(q)].astype(F32).reshape(256, 128)
                for part in range(2):
                    stack = [yf[q, pl.ds(part * 4 + m, 32, stride=8), :] for m in range(4)]
                    turned = jnp.transpose(jnp.concatenate(stack, axis=0)).astype(BF16)
                    for m in range(4):
                        for j in range(4):
                            first = (q * 4 + j) * 128 + m * 32
                            zt[m * 64 + part * 32:m * 64 + part * 32 + 32, first:first + 32] = (
                                turned[j * 32:j * 32 + 32, m * 32:m * 32 + 32]
                            )
            if i == 0:
                early = slice(0, piece[1] * 512)
                late = slice(piece[1] * 512, 1536)
                back[...] = dot(zt[:, early], wp[early, :])
        sent(gs, 0)
        for piece in PIECES[2]:
            block = columns(piece)
            width = (piece[1] - piece[0]) * 128
            term = (0.25 * (back[:, block] + dot(zt[:, late], wp[late, block]))).astype(BF16).astype(F32)
            total = (spec[:, :, block].reshape(256, width) + term).astype(BF16).astype(F32)
            for q in range(*piece):
                parts = [total[j * 16:j * 16 + 16, cols(q - piece[0])] for j in range(16)]
                for j, part in enumerate(by_holder(parts)):
                    rs[j, :, cols(q)] = part.astype(BF16)
            send(rs, c, 2, piece[1])
        sent(ms, 1)
        pl.when(n == 0)(loads[10].wait)

        for piece in units(PIECES[2], PIECES[3]):
            arrive(c, 2, piece[0])
            for q in range(*piece):
                right = c[:, :, cols(q)].reshape(256, 128)
                solved = dot(inv[q * 8], right)
                for j in range(1, 8):
                    solved = jnp.where((((lane128 + row) & 127) >> 4) == j, dot(inv[q * 8 + j], right), solved)
                us[:, :, cols(q)] = solved.astype(BF16).reshape(NROW, 16, 128)
            send(us, s, 3, piece[1])
        sent(rs, 2)
        for piece in PIECES[3]:
            arrive(s, 3, piece[0])
            for q in range(*piece):
                for j, part in enumerate(by_component([s[j, :, cols(q)].astype(F32) for j in range(16)])):
                    spec[j, :, cols(q)] = part
                    xs[j, :, cols(q)] = part.astype(BF16)
        sent(us, 3)
        return 0

    lax.fori_loop(0, STEPS, step, 0)


def unload_kernel(xs, z, out_a, out_b, out_z):
    from_degree = onehot(degree_of(iota((N, N), 0)) == iota((N, N), 1))
    result = dot(xs[...].reshape(256, N), from_degree)
    for m in range(4):
        for part in range(2):
            for f, out in ((0, out_a), (1, out_b)):
                i = m * 4 + part * 2 + f
                out[:, part, m, :] = result[i * 16:i * 16 + 16]
    lane = iota((16, N), 1)
    spread = jnp.where((lane & 31) == iota((16, N), 0), jnp.broadcast_to(z[0:1, :], (16, N)), 0.0)
    out_z[...] = exact_dot(spread, onehot((iota((N, 12), 0) >> 5) == iota((N, 12), 1)))


def shards(
    field_a, field_b, mode_ids, legendre, quad_weights, colat_cos, lorentz, theta_order, inverse
):
    vmem = pl.BlockSpec(memory_space=pltpu.VMEM)
    hbm = pl.BlockSpec(memory_space=pltpu.HBM)
    xs, z = pl.pallas_call(
        kernel,
        out_shape=(
            jax.ShapeDtypeStruct((16, 16, N), BF16),
            jax.ShapeDtypeStruct((8, N), F32),
        ),
        in_specs=[hbm] * 9,
        out_specs=(vmem, vmem),
        scratch_shapes=[
            pltpu.VMEM((16, 2, 4, N), F32),
            pltpu.VMEM((16, 2, 4, N), F32),
            pltpu.VMEM((4, N, N), BF16),
            pltpu.VMEM((16, N), F32),
            pltpu.SMEM((128,), jnp.int32),
            pltpu.SMEM((N,), jnp.int32),
            pltpu.VMEM((128,), jnp.int32),
            pltpu.VMEM((N,), jnp.int32),
            pltpu.VMEM((N,), F32),
            pltpu.VMEM((N,), F32),
            pltpu.VMEM((4, N, N), BF16),
            pltpu.VMEM((1536, N), BF16),
            pltpu.VMEM((16, 16, N), F32),
            pltpu.VMEM((NPHI, 256), BF16),
            pltpu.VMEM((256, NPHI), BF16),
            pltpu.VMEM((NPHI, 256), F32),
            pltpu.VMEM((1, N), F32),
            pltpu.VMEM((1, N), F32),
            pltpu.VMEM((NPHI, N), BF16),
            pltpu.VMEM((3, 256, 128), F32),
            pltpu.VMEM((256, 1536), BF16),
            pltpu.VMEM((256, N), F32),
            pltpu.VMEM((NMA, 8, N), BF16),
            pltpu.VMEM((NMA, 8, N), BF16),
            pltpu.VMEM((NMA, 8, N), BF16),
            pltpu.VMEM((NMA, 8, N), BF16),
            pltpu.VMEM((NROW, 16, N), BF16),
            pltpu.VMEM((NROW, 16, N), BF16),
            pltpu.VMEM((NROW, 16, N), BF16),
            pltpu.VMEM((NROW, 16, N), BF16),
            pltpu.VMEM((24, 256, 256), BF16),
            pltpu.VMEM((N, N), BF16),
            pltpu.SemaphoreType.DMA((4, 3)),
            pltpu.SemaphoreType.DMA((4, 3)),
            pltpu.SemaphoreType.DMA((11,)),
        ],
        compiler_params=pltpu.CompilerParams(
            collective_id=0, has_side_effects=True, vmem_limit_bytes=64 * 1024 * 1024
        ),
        name="shell_steps",
    )(
        field_a, field_b, mode_ids, theta_order, legendre, quad_weights, colat_cos, lorentz, inverse,
    )
    return pl.pallas_call(
        unload_kernel,
        out_shape=(
            jax.ShapeDtypeStruct((16, 2, 4, N), F32),
            jax.ShapeDtypeStruct((16, 2, 4, N), F32),
            jax.ShapeDtypeStruct((16, 12), F32),
        ),
        in_specs=[vmem, vmem],
        out_specs=(vmem, vmem, vmem),
        compiler_params=pltpu.CompilerParams(vmem_limit_bytes=64 * 1024 * 1024),
        name="unload",
    )(xs, z)


def solution(mesh):
    return jax.shard_map(
        shards,
        mesh=mesh,
        in_specs=(
            P("row", None, "ma", None),
            P("row", None, "ma", None),
            P(),
            P("ma", None, None),
            P(),
            P(),
            P("row", None),
            P(),
            P("row", None, None),
        ),
        out_specs=(P("row", None, "ma", None), P("row", None, "ma", None), P("row", "ma")),
        check_vma=False,
    )
```

```python
import math

import jax
import jax.numpy as jnp
from jax import lax
from jax.experimental import pallas as pl
from jax.experimental.pallas import tpu as pltpu
from jax.sharding import PartitionSpec as P

STEPS = 3
NPHI = 768
N = 384
NMA = 32
NROW = 16
PIECES = (((0, 1), (1, 3)), ((0, 1), (1, 3)), ((0, 1), (1, 3)), ((0, 1), (1, 3)))
F32 = jnp.float32
BF16 = jnp.bfloat16
MESH = pl.DeviceIdType.MESH


def iota(shape, dim):
    return lax.broadcasted_iota(jnp.int32, shape, dim)


def dot(a, b):
    return jnp.dot(a, b, preferred_element_type=F32)


def degree_of(column):
    holder = -column & 15
    return holder * 24 + (column >> 7) * 8 + ((((column & 127) + holder) >> 4) & 7)


def onehot(test):
    return jnp.where(test, 1.0, 0.0).astype(BF16)


def exact_dot(a, hot):
    hi = a.astype(BF16)
    rest = a - hi.astype(F32)
    mid = rest.astype(BF16)
    low = (rest - mid.astype(F32)).astype(BF16)
    return dot(hi, hot) + dot(mid, hot) + dot(low, hot)


def far_first(count):
    return sorted(range(count), key=lambda d: -min(d, count - d))


def farthest(first, second):
    pairs = [(a, b) for a in far_first(first) for b in far_first(second)]
    pairs.sort(key=lambda p: -min(p[0], first - p[0]) - min(p[1], second - p[1]))
    return pairs[:-1]


def units(arriving, leaving):
    cuts = sorted({low for low, _ in arriving + leaving}) + [3]
    return list(zip(cuts, cuts[1:]))


def kernel(
    fa_hbm, fb_hbm, ids_hbm, theta_hbm, leg_hbm, qw_hbm, colat_hbm, lor_hbm, inv_hbm,
    xs, out_z,
    fa, fb, leg, lor, ids_s, theta_s, ids_v, theta_v, qw, colat,
    legp, wp, spec, tt, bt, val, k1, k2, force, yf, zt, back, gs, g, ms, h, rs, c, us, s, inv, pick,
    send_sem, recv_sem, load_sem,
):
    row = lax.axis_index("row")
    ma = lax.axis_index("ma")
    ma_x, ma_z = ma // 8, lax.rem(ma, 8)
    row_y, row_core = row // 2, lax.rem(row, 2)
    on_x = [lax.rem(ma_x + d, 4) * 8 for d in range(4)]
    on_z = [lax.rem(ma_z + d, 8) for d in range(8)]
    on_y = [lax.rem(row_y + d, 8) * 2 for d in range(8)]
    on_core = [row_core, 1 - row_core]
    ma_others = [on_x[a] + on_z[b] for a, b in farthest(4, 8)]
    row_others = [on_y[a] + on_core[b] for a in far_first(8) for b in (1, 0) if (a, b) != (0, 0)]

    barrier = pltpu.get_barrier_semaphore()
    for to in ma_others:
        pl.semaphore_signal(barrier, inc=1, device_id={"ma": to}, device_id_type=MESH)
    for to in row_others:
        pl.semaphore_signal(barrier, inc=1, device_id={"row": to}, device_id_type=MESH)

    loads = [
        pltpu.make_async_copy(src, dst, load_sem.at[i])
        for i, (src, dst) in enumerate((
            (theta_hbm, theta_v), (leg_hbm, leg), (ids_hbm, ids_s), (fa_hbm, fa), (fb_hbm, fb), (theta_hbm, theta_s),
            (ids_hbm, ids_v), (colat_hbm, colat), (lor_hbm, lor), (qw_hbm, qw), (inv_hbm, inv),
        ))
    ]
    for load in loads:
        load.start()

    lane = iota((1, N), 1)
    lane128 = iota((1, 128), 1)
    degree = degree_of(lane)

    shuffle = onehot(iota((N, N), 0) == (lane & 31) * 12 + (lane >> 5))
    loads[0].wait()
    nat = onehot(iota((N, N), 0) == theta_v[...].reshape(1, N))
    pick[...] = jnp.transpose(dot(nat, shuffle)).astype(BF16)
    for load in loads[1:5]:
        load.wait()
    for m in range(4):
        legp[m] = dot(pick[...], leg[m]).astype(BF16)
        alive = lane >= ids_s[ma * 4 + m]
        for part in range(2):
            for f, field in ((0, fa), (1, fb)):
                xs[m * 4 + part * 2 + f] = jnp.where(alive, field[:, part, m, :], 0.0).astype(BF16)

    pl.semaphore_wait(barrier, NMA + NROW - 2)

    def cols(q):
        return slice(q * 128, q * 128 + 128)

    def columns(piece):
        return slice(piece[0] * 128, piece[1] * 128)

    def send(src, dst, k, done):
        axis, me, others = ("ma", ma, ma_others) if k < 2 else ("row", row, row_others)
        for i, piece in enumerate(PIECES[k]):
            if piece[1] == done:
                block = columns(piece)
                for to in others:
                    pltpu.make_async_remote_copy(
                        src_ref=src.at[to, :, block],
                        dst_ref=dst.at[me, :, block],
                        send_sem=send_sem.at[k, i],
                        recv_sem=recv_sem.at[k, i],
                        device_id={axis: to},
                        device_id_type=MESH,
                    ).start()
                dst[me, :, block] = src[me, :, block]

    def finish(ref, sem, piece):
        rest = ref.at[pl.ds(0, ref.shape[0] - 1), :, columns(piece)]
        pltpu.make_async_copy(rest, rest, sem).wait()

    def arrive(dst, k, first):
        for i, piece in enumerate(PIECES[k]):
            if piece[0] == first:
                finish(dst, recv_sem.at[k, i], piece)

    def sent(src, k):
        for i, piece in enumerate(PIECES[k]):
            finish(src, send_sem.at[k, i], piece)

    def by_holder(parts):
        parts = [pltpu.roll(v, i, 1) if i else v for i, v in enumerate(parts)]
        for k in (1, 2, 4, 8):
            parts = [jnp.where((lane128 & k) == 0, parts[j], parts[(j + k) % 16]) for j in range(16)]
        return parts

    def by_component(parts):
        for k in (1, 2, 4, 8):
            parts = [jnp.where((lane128 & k) == 0, parts[i], parts[(i - k) % 16]) for i in range(16)]
        return [pltpu.roll(v, 128 - i, 1) if i else v for i, v in enumerate(parts)]

    def to_degree():
        return onehot(iota((N, N), 0) == degree)

    def prepare_spectral():
        hot = to_degree()
        for m in range(4):
            alive = lane >= ids_s[ma * 4 + m]
            for part in range(2):
                for f, field in ((0, fa), (1, fb)):
                    piece = jnp.where(alive, field[:, part, m, :], 0.0)
                    hi = piece.astype(BF16)
                    lo = (piece - hi.astype(F32)).astype(BF16)
                    spec[m * 4 + part * 2 + f] = dot(hi, hot) + dot(lo, hot)

    def prepare_synthesis():
        hot = to_degree()
        for m in range(4):
            legp[m] = dot(legp[m], hot).astype(BF16)

    def prepare_longitude():
        for load in loads[5:9]:
            load.wait()
        n = iota((1, 256), 1)
        expand = onehot(iota((128, 256), 0) == (n >> 3) * 4 + (n & 3))
        ids = jnp.broadcast_to(ids_v[...].reshape(1, 128), (8, 128))
        top = ids >> 4
        mode = 16.0 * dot(top.astype(F32).astype(BF16), expand) + dot((ids & 15).astype(F32).astype(BF16), expand)
        mode = mode[0:1]

        def angles(count, period):
            k = mode * iota((count, 256), 0).astype(F32)
            k = k - period * jnp.floor((k + 0.5) * (1.0 / period))
            k = jnp.where(k > period / 2, k - period, k)
            return k * (2.0 * math.pi / period)

        coarse = angles(24, 24)
        fine = angles(32, NPHI)
        cos_c, sin_c = jnp.cos(coarse), jnp.sin(coarse)
        cos_f, sin_f = jnp.cos(fine), jnp.sin(fine)
        is_cos = (n & 4) == 0
        lead_c = jnp.where(is_cos, cos_c, -sin_c)
        lead_s = jnp.where(is_cos, sin_c, cos_c)
        for a in range(24):
            value = lead_c[a:a + 1] * cos_f - lead_s[a:a + 1] * sin_f
            val[a * 32:a * 32 + 32, :] = value
            tt[a * 32:a * 32 + 32, :] = (value * (1.0 / math.sqrt(128))).astype(BF16)
        for a in range(3):
            bt[:, a * 256:a * 256 + 256] = (
                jnp.transpose(val[a * 256:a * 256 + 256, :]) * math.sqrt(2.0 / NPHI)
            ).astype(BF16)

        own = jnp.zeros((1, N), jnp.int32)
        for t in range(12):
            own = jnp.where((lane >> 5) == t, theta_s[ma * 12 + t], own)
        hot = onehot(iota((N, N), 0) == own)
        is_a = (lane & 16) == 0
        cosines = exact_dot(jnp.broadcast_to(colat[...].reshape(1, N), (8, N)), hot)[0:1]
        k1[...] = jnp.where(is_a, 2.0 * cosines, -2.0 * cosines)
        energy = exact_dot(lor[...], hot)
        energy = jnp.sum(jnp.where(iota((16, N), 0) == (lane & 15), energy, 0.0), axis=0, keepdims=True)
        k2[...] = jnp.where(is_a, energy, 1.0)

    def prepare_weighted():
        loads[9].wait()
        hot = to_degree()
        column = jnp.transpose(jnp.broadcast_to(qw[...].reshape(1, N), (128, N)))[:, 0:1]
        for m in range(4):
            w = (column * leg[m].astype(F32)).astype(BF16)
            w = dot(pick[...], dot(w, hot).astype(BF16))
            w = jnp.where(degree >= ids_s[ma * 4 + m], w, 0.0).astype(BF16)
            for t in range(12):
                wp[t * 128 + m * 32:t * 128 + m * 32 + 32, :] = w[t * 32:t * 32 + 32]

    zt[...] = jnp.zeros_like(zt)

    def step(n, _):
        for piece in PIECES[0]:
            low, high = piece
            for m in range(4):
                x0 = xs[m * 4:m * 4 + 2].reshape(32, N)
                x1 = xs[m * 4 + 2:m * 4 + 4].reshape(32, N)
                x = jnp.concatenate([x0] * 4 + [x1] * 4, axis=0)
                y = lax.dot_general(
                    legp[m, columns(piece), :], x, (((1,), (1,)), ((), ())), preferred_element_type=F32
                )
                for part in range(2):
                    for q in range(low, high):
                        first = (q - low) * 128
                        block = y[first:first + 32, cols(part)]
                        for j in range(1, 4):
                            other = y[first + j * 32:first + j * 32 + 32, cols(part)]
                            block = jnp.where((lane128 >> 5) == j, other, block)
                        yf[q, pl.ds(part * 4 + m, 32, stride=8), :] = block
            for q in range(low, high):
                gs[:, :, cols(q)] = yf[q].reshape(NMA, 8, 128).astype(BF16)
            send(gs, g, 0, high)
        pl.when(n == 0)(prepare_longitude)
        pl.when(n == 0)(prepare_spectral)

        for piece in units(PIECES[0], PIECES[1]):
            arrive(g, 0, piece[0])
            width = (piece[1] - piece[0]) * 128
            block = columns(piece)
            grids = [g[:, :, cols(q)].astype(F32).reshape(256, 128) for q in range(*piece)]
            others = [
                jnp.where((lane128 & 16) == 0, pltpu.roll(v, 112, 1), pltpu.roll(v, 16, 1)) for v in grids
            ]
            both = jnp.concatenate(grids + others, axis=1).astype(BF16)
            total = jnp.zeros((1, width), F32)
            for a in range(3):
                phys = dot(tt[a * 256:a * 256 + 256, :], both)
                value = phys[:, width:] * (k1[:, block] + k2[:, block] * phys[:, :width])
                force[a * 256:a * 256 + 256, block] = value.astype(BF16)
                total = total + jnp.sum(value, axis=0, keepdims=True)
            out_z[:, block] = jnp.broadcast_to(total * (1.0 / NPHI), (8, width))
            ms[:, :, block] = dot(bt[...], force[:, block]).reshape(NMA, 8, width).astype(BF16)
            send(ms, h, 1, piece[1])
        pl.when(n == 0)(prepare_weighted)

        for i, piece in enumerate(PIECES[1]):
            arrive(h, 1, piece[0])
            for q in range(*piece):
                yf[q] = h[:, :, cols(q)].astype(F32).reshape(256, 128)
                for part in range(2):
                    stack = [yf[q, pl.ds(part * 4 + m, 32, stride=8), :] for m in range(4)]
                    turned = jnp.transpose(jnp.concatenate(stack, axis=0)).astype(BF16)
                    for m in range(4):
                        for j in range(4):
                            first = (q * 4 + j) * 128 + m * 32
                            zt[m * 64 + part * 32:m * 64 + part * 32 + 32, first:first + 32] = (
                                turned[j * 32:j * 32 + 32, m * 32:m * 32 + 32]
                            )
            if i == 0:
                early = slice(0, piece[1] * 512)
                late = slice(piece[1] * 512, 1536)
                back[...] = dot(zt[:, early], wp[early, :])
        sent(gs, 0)
        for piece in PIECES[2]:
            block = columns(piece)
            width = (piece[1] - piece[0]) * 128
            term = (0.25 * (back[:, block] + dot(zt[:, late], wp[late, block]))).astype(BF16).astype(F32)
            total = (spec[:, :, block].reshape(256, width) + term).astype(BF16).astype(F32)
            for q in range(*piece):
                parts = [total[j * 16:j * 16 + 16, cols(q - piece[0])] for j in range(16)]
                for j, part in enumerate(by_holder(parts)):
                    rs[j, :, cols(q)] = part.astype(BF16)
            send(rs, c, 2, piece[1])
        sent(ms, 1)
        pl.when(n == 0)(prepare_synthesis)
        pl.when(n == 0)(loads[10].wait)

        for piece in units(PIECES[2], PIECES[3]):
            arrive(c, 2, piece[0])
            for q in range(*piece):
                right = c[:, :, cols(q)].reshape(256, 128)
                solved = dot(inv[q * 8], right)
                for j in range(1, 8):
                    solved = jnp.where((((lane128 + row) & 127) >> 4) == j, dot(inv[q * 8 + j], right), solved)
                us[:, :, cols(q)] = solved.astype(BF16).reshape(NROW, 16, 128)
            send(us, s, 3, piece[1])
        sent(rs, 2)
        for piece in PIECES[3]:
            arrive(s, 3, piece[0])
            for q in range(*piece):
                for j, part in enumerate(by_component([s[j, :, cols(q)].astype(F32) for j in range(16)])):
                    spec[j, :, cols(q)] = part
                    xs[j, :, cols(q)] = part.astype(BF16)
        sent(us, 3)
        return 0

    lax.fori_loop(0, STEPS, step, 0)


def unload_kernel(xs, z, out_a, out_b, out_z):
    from_degree = onehot(degree_of(iota((N, N), 0)) == iota((N, N), 1))
    result = dot(xs[...].reshape(256, N), from_degree)
    for m in range(4):
        for part in range(2):
            for f, out in ((0, out_a), (1, out_b)):
                i = m * 4 + part * 2 + f
                out[:, part, m, :] = result[i * 16:i * 16 + 16]
    lane = iota((16, N), 1)
    spread = jnp.where((lane & 31) == iota((16, N), 0), jnp.broadcast_to(z[0:1, :], (16, N)), 0.0)
    out_z[...] = exact_dot(spread, onehot((iota((N, 12), 0) >> 5) == iota((N, 12), 1)))


def shards(
    field_a, field_b, mode_ids, legendre, quad_weights, colat_cos, lorentz, theta_order, inverse
):
    vmem = pl.BlockSpec(memory_space=pltpu.VMEM)
    hbm = pl.BlockSpec(memory_space=pltpu.HBM)
    xs, z = pl.pallas_call(
        kernel,
        out_shape=(
            jax.ShapeDtypeStruct((16, 16, N), BF16),
            jax.ShapeDtypeStruct((8, N), F32),
        ),
        in_specs=[hbm] * 9,
        out_specs=(vmem, vmem),
        scratch_shapes=[
            pltpu.VMEM((16, 2, 4, N), F32),
            pltpu.VMEM((16, 2, 4, N), F32),
            pltpu.VMEM((4, N, N), BF16),
            pltpu.VMEM((16, N), F32),
            pltpu.SMEM((128,), jnp.int32),
            pltpu.SMEM((N,), jnp.int32),
            pltpu.VMEM((128,), jnp.int32),
            pltpu.VMEM((N,), jnp.int32),
            pltpu.VMEM((N,), F32),
            pltpu.VMEM((N,), F32),
            pltpu.VMEM((4, N, N), BF16),
            pltpu.VMEM((1536, N), BF16),
            pltpu.VMEM((16, 16, N), F32),
            pltpu.VMEM((NPHI, 256), BF16),
            pltpu.VMEM((256, NPHI), BF16),
            pltpu.VMEM((NPHI, 256), F32),
            pltpu.VMEM((1, N), F32),
            pltpu.VMEM((1, N), F32),
            pltpu.VMEM((NPHI, N), BF16),
            pltpu.VMEM((3, 256, 128), F32),
            pltpu.VMEM((256, 1536), BF16),
            pltpu.VMEM((256, N), F32),
            pltpu.VMEM((NMA, 8, N), BF16),
            pltpu.VMEM((NMA, 8, N), BF16),
            pltpu.VMEM((NMA, 8, N), BF16),
            pltpu.VMEM((NMA, 8, N), BF16),
            pltpu.VMEM((NROW, 16, N), BF16),
            pltpu.VMEM((NROW, 16, N), BF16),
            pltpu.VMEM((NROW, 16, N), BF16),
            pltpu.VMEM((NROW, 16, N), BF16),
            pltpu.VMEM((24, 256, 256), BF16),
            pltpu.VMEM((N, N), BF16),
            pltpu.SemaphoreType.DMA((4, 3)),
            pltpu.SemaphoreType.DMA((4, 3)),
            pltpu.SemaphoreType.DMA((11,)),
        ],
        compiler_params=pltpu.CompilerParams(
            collective_id=0, has_side_effects=True, vmem_limit_bytes=64 * 1024 * 1024
        ),
        name="shell_steps",
    )(
        field_a, field_b, mode_ids, theta_order, legendre, quad_weights, colat_cos, lorentz, inverse,
    )
    return pl.pallas_call(
        unload_kernel,
        out_shape=(
            jax.ShapeDtypeStruct((16, 2, 4, N), F32),
            jax.ShapeDtypeStruct((16, 2, 4, N), F32),
            jax.ShapeDtypeStruct((16, 12), F32),
        ),
        in_specs=[vmem, vmem],
        out_specs=(vmem, vmem, vmem),
        compiler_params=pltpu.CompilerParams(vmem_limit_bytes=64 * 1024 * 1024),
        name="unload",
    )(xs, z)


def solution(mesh):
    return jax.shard_map(
        shards,
        mesh=mesh,
        in_specs=(
            P("row", None, "ma", None),
            P("row", None, "ma", None),
            P(),
            P("ma", None, None),
            P(),
            P(),
            P("row", None),
            P(),
            P("row", None, None),
        ),
        out_specs=(P("row", None, "ma", None), P("row", None, "ma", None), P("row", "ma")),
        check_vma=False,
    )
```
